32 devices in a mesh: jpair: 2 (over x), blk: 16 (over z, y, core).
Axes of the slice: x: 2, y: 2, z: 4, core: 2. Of those that a mesh axis runs over, the one named last changes fastest.
Arguments:
- dipole: bfloat16 [256, 12, 3, 256, 256], P('blk'), may hold values from -24 to 24
- block_cols: int32 [256, 12], P('blk'), may hold values from 0 to 255, as said below
- upper_vecs: bfloat16 [131072, 256], P(('jpair', 'blk')), parts along dimension 0, may hold values from -0.0234375 to 0.0234375
- lower_vecs: bfloat16 [131072, 128], P(('jpair', 'blk')), parts along dimension 0, may hold values from -0.0234375 to 0.0234375
- upper_energy: float32 [512], P('jpair'), parts along dimension 0, may hold values from 1 to 2
- lower_energy: float32 [256], P('jpair'), parts along dimension 0, may hold values from 0 to 0.8
Outputs:
- strength: float32 [512, 128], P(('jpair', 'blk')), parts along dimension 0
- intensity: float32 [512, 128], P(('jpair', 'blk')), parts along dimension 0
The draws below stay inside these ranges and needn't reach their ends.
There are 2 independent parts, one for each index of `jpair`. The reference program is written for one: setup_inputs(seed, part) draws one part's arguments, and reference() takes and returns one part's arrays. A program takes and returns all parts, laid end to end along the dimension named above; an argument that names none is the same for every part. Nothing has to cross between parts.
Inputs may be any that keep to these rules, and one draw needn't show every extreme that they name: `block_cols`: within one block row the 12 block columns are distinct, and one of them is the row's own index. Splitting the block rows into 16 equal runs of consecutive rows, the columns of one run that fall in another run number at most 12 distinct blocks for each other run, and exactly 12 for some.
All inputs are finite; a program needn't handle non-finite values.
Results may differ from the reference program's by a relative error of at most 0.0026.
Values may be sent and summed in bfloat16 or wider, within the bound.
No kernel may reach another device: no remote copies, remote signals or barrier semaphores. Data moves between devices by JAX's collectives and lax.ppermute only.
A program may use at most 256 MiB of HBM per device.

```python
import jax
import jax.numpy as jnp
from jax import lax

NB = 65536
BS = 256
NZ = 12
NU = 256
NL = 128
NBR = 256
N_BLK = 16


def draw_block_cols(key, part):
    per_dev = NBR // N_BLK
    others = N_BLK - 1
    slots = (NZ - 1) * per_dev

    def one_device(device):
        dev_key = jax.random.fold_in(key, device)
        order = jax.random.permutation(jax.random.fold_in(dev_key, 1), others).astype(jnp.int32) + 1
        starts = jax.random.randint(jax.random.fold_in(dev_key, 2), (others,), 0, per_dev).astype(jnp.int32)
        slot_ids = jnp.arange(slots, dtype=jnp.int32)
        which = slot_ids % others
        copy_num = slot_ids // others
        owner = (device + order[which]) % N_BLK
        local_id = (starts[which] + copy_num) % per_dev
        picked = (owner * per_dev + local_id).reshape(NZ - 1, per_dev).T
        own_ids = device * per_dev + jnp.arange(per_dev, dtype=jnp.int32)
        return jnp.concatenate([own_ids[:, None], picked], axis=1)
    device_ids = jnp.arange(N_BLK, dtype=jnp.int32)
    return jax.vmap(one_device)(device_ids).reshape(NBR, NZ).astype(jnp.int32)


def levels(stream_key, extent, split, smallest, high):
    level, own = 1.0, jax.random.fold_in(stream_key, 6)
    for position, shards_of in split:
        draws = jnp.exp(jax.random.uniform(jax.random.fold_in(own, position), (shards_of,), jnp.float32, smallest / len(split), high / len(split)))
        level = level * jnp.repeat(draws, extent[position] // shards_of).reshape([-1 if axis == position else 1 for axis in range(len(extent))])
    return level


def noise(rng, extent, width, most, cuts=(), kind=jnp.bfloat16):
    entries = width * jax.random.normal(rng, extent, jnp.float32)
    if cuts:
        entries = entries * levels(rng, extent, cuts, -0.22, 0.18)
    return jnp.clip(entries, -most, most).astype(kind)


def setup_inputs(seed: int = 0, part: int = 0) -> dict:
    keys = jax.random.split(jax.random.key(seed), 7)
    own_keys = jax.random.split(jax.random.fold_in(keys[6], part), 7)
    dipole = noise(keys[0], (NBR, NZ, 3, BS, BS), 4.0, 24.0, ((0, 16),))
    block_cols = draw_block_cols(jax.random.fold_in(keys[6], 71), part)
    upper_vecs = noise(own_keys[2], (NB, NU), NB ** -0.5, 0.0234375, ((0, 16),))
    lower_vecs = noise(own_keys[3], (NB, NL), NB ** -0.5, 0.0234375, ((0, 16),))
    upper_energy = jnp.clip(jax.random.uniform(own_keys[4], (NU,), jnp.float32, 1.0, 2.0), 1.0, 2.0)
    lower_energy = jnp.clip(jax.random.uniform(own_keys[5], (NL,), jnp.float32, 0.0, 0.8), 0.0, 0.8)
    return {"dipole": dipole, "block_cols": block_cols, "upper_vecs": upper_vecs, "lower_vecs": lower_vecs, "upper_energy": upper_energy, "lower_energy": lower_energy}


THERMAL = 0.3


def reference(dipole, block_cols, upper_vecs, lower_vecs, upper_energy, lower_energy):
    upper_blocks = upper_vecs.reshape(NBR, BS, NU)
    lower_blocks = lower_vecs.reshape(NBR, BS, NL)

    def one_row(running, row_inputs):
        dip_blocks, col_ids, up_rows = row_inputs
        halves = jnp.einsum("kast,su->katu", dip_blocks.astype(jnp.float32), up_rows.astype(jnp.float32)).astype(jnp.bfloat16)
        low_rows = lower_blocks[col_ids.astype(jnp.int32)]
        running = running + jnp.einsum("katu,ktl->aul", halves.astype(jnp.float32), low_rows.astype(jnp.float32))
        return running, None

    start_sum = jnp.zeros((3, NU, NL), jnp.float32)
    proj, _ = lax.scan(one_row, start_sum, (dipole, block_cols, upper_blocks))
    strength = jnp.sum(proj * proj, axis=0)
    wavenumber = upper_energy[:, None] - lower_energy[None, :]
    intensity = wavenumber ** 3 * jnp.exp(-lower_energy / THERMAL)[None, :] * strength
    return strength, intensity
```

```python
import functools

import jax
import jax.numpy as jnp
from jax import lax
from jax.experimental import pallas as pl
from jax.experimental.pallas import tpu as pltpu
from jax.sharding import PartitionSpec as P

THERMAL = 0.3
SLOTS = 32
FIRST_SLOTS = 16
GROUP = 4
ENTRY_BITS = 5

VMEM = pl.BlockSpec(memory_space=pltpu.VMEM)
SMEM = pl.BlockSpec(memory_space=pltpu.SMEM)
ANY = pl.BlockSpec(memory_space=pl.ANY)


def stage_body(stage, first, reach, layout, n_pieces, n_extra, *refs):
    plan_in, dipole = refs[:2]
    pieces = refs[2 : 2 + n_pieces]
    refs = refs[2 + n_pieces + n_extra :]
    if not first:
        refs = refs[2:]
    moments, entries, _, plan, low, plan_sem, entry_sems, piece_sems = refs
    n_slots, comps, block, _ = entries.shape
    total, low_bits = layout

    plan_copy = pltpu.make_async_copy(plan_in, plan, plan_sem)
    plan_copy.start()
    offset = 0
    piece_copies = []
    for i, piece in enumerate(pieces):
        count = piece.shape[0]
        piece_copies.append(
            pltpu.make_async_copy(piece, low.at[pl.ds(offset, count)], piece_sems.at[i])
        )
        offset += count
    for copy in piece_copies:
        copy.start()
    if first:
        moments[...] = jnp.zeros_like(moments)
    blank = low.shape[0] - 1
    low[blank] = jnp.zeros(low.shape[1:], low.dtype)
    plan_copy.wait()

    begin = plan[total + stage]
    end = plan[total + stage + 1]
    ahead = jnp.minimum(begin + reach[stage], total)
    if first:
        ready = begin
    else:
        ready = jnp.maximum(jnp.minimum(plan[total + stage - 1] + reach[stage - 1], total), begin)

    def place(pos):
        return pos & (n_slots - 1) if n_slots & (n_slots - 1) == 0 else lax.rem(pos, n_slots)

    def row(code):
        return code >> (low_bits + ENTRY_BITS)

    def load(pos):
        code = plan[pos]
        slot = place(pos)
        entry = (code >> low_bits) & ((1 << ENTRY_BITS) - 1)
        return pltpu.make_async_copy(dipole.at[row(code), entry], entries.at[slot], entry_sems.at[slot])

    @pl.loop(ready, ahead)
    def _(pos):
        load(pos).start()

    for copy in piece_copies:
        copy.wait()

    def work(start):
        positions = [start + i for i in range(GROUP)]

        @pl.when(start + GROUP > ready)
        def _():
            for pos in positions:
                @pl.when((pos >= ready) & (pos < end))
                def _(pos=pos):
                    load(pos).wait()

        kept = [jnp.minimum(pos, end - 1) for pos in positions]
        codes = [plan[pos] for pos in kept]
        rows = [row(code) for code in codes]
        picks = [
            jnp.where(pos < end, code & ((1 << low_bits) - 1), blank) for pos, code in zip(positions, codes)
        ]
        blocks = [low[pick] for pick in picks]
        for a in range(comps):
            products = [
                jnp.dot(entries[place(pos), a], lower, preferred_element_type=jnp.float32)
                for pos, lower in zip(kept, blocks)
            ]
            for r, product in zip(rows, products):
                moments[r, pl.ds(a * block, block)] += product

        @pl.when(start + n_slots < end)
        def _():
            for pos in positions:
                @pl.when(pos + n_slots < end)
                def _(pos=pos):
                    load(pos + n_slots).start()

    if pieces:
        @pl.loop(0, (end - begin + GROUP - 1) // GROUP)
        def _(g):
            work(begin + g * GROUP)

    @pl.loop(jnp.maximum(ready, end), ahead)
    def _(pos):
        load(pos).wait()


def split_halves(sums, bits, level, keep, send):
    comps, count, share, lower_count = sums.shape
    halves = sums.reshape(comps, count // 2, 2, share, lower_count)
    side = jnp.broadcast_to(bits[level][None, None, :1], (comps, count // 2, share, lower_count)) > 0
    keep[...] = jnp.where(side, halves[:, :, 1], halves[:, :, 0])
    send[...] = jnp.where(side, halves[:, :, 0], halves[:, :, 1])


def project(upper_t, moments, comps, lay):
    rows, height, _ = moments.shape
    block = height // comps
    span = min(4, rows)
    sums = []
    for a in range(comps):
        acc = None
        for r in range(0, rows, span):
            parts = [moments[r + i, pl.ds(a * block, block)] for i in range(span)]
            wide = jnp.concatenate(parts, axis=0)
            high = wide.astype(jnp.bfloat16)
            rest = (wide - high.astype(jnp.float32)).astype(jnp.bfloat16)
            both = jnp.concatenate([high, rest], axis=1)
            term = jnp.dot(
                upper_t[:, pl.ds(r * block, span * block)], both, preferred_element_type=jnp.float32
            )
            acc = term if acc is None else acc + term
        half = acc.shape[1] // 2
        sums.append((acc[:, :half] + acc[:, half:]).reshape(lay + (half,)))
    return jnp.stack(sums)


def small_call(body, out_shape, *operands):
    return pl.pallas_call(
        body,
        out_shape=out_shape,
        in_specs=[VMEM] * len(operands),
        out_specs=jax.tree.map(lambda _: VMEM, out_shape),
        compiler_params=pltpu.CompilerParams(vmem_limit_bytes=8 * 2**20),
    )(*operands)


def own_outputs(upper_t, moments, comps, bits, factor, group):
    upper_count = upper_t.shape[0]
    lower_count = moments.shape[2]
    share = upper_count // group
    levels = bits.shape[0]

    def shapes(count):
        return [jax.ShapeDtypeStruct((comps, count, share, lower_count), jnp.float32)] * 2

    def first(upper_t, moments, bits, keep, send):
        split_halves(project(upper_t, moments, comps, (group, share)), bits, 0, keep, send)

    def middle(level, held, other, bits, keep, send):
        split_halves(held[...] + other[...], bits, level, keep, send)

    def final(held, other, factor, strength, intensity):
        own = (held[...] + other[...])[:, 0]
        strength[...] = jnp.sum(own * own, axis=0)
        intensity[...] = factor[...] * strength[...]

    keep, send = small_call(first, shapes(group // 2), upper_t, moments, bits)
    for level in range(levels):
        bit = 1 << level
        other = lax.ppermute(send, "blk", [(d, d ^ bit) for d in range(group)])
        if level + 1 < levels:
            count = group >> (level + 2)
            keep, send = small_call(
                functools.partial(middle, level + 1), shapes(count), keep, other, bits
            )
    out = [jax.ShapeDtypeStruct((share, lower_count), jnp.float32)] * 2
    return small_call(final, out, keep, other, factor)


def run_stage(stage, reach, plan, layout, dipole, pieces, lower_count, state, needed=()):
    rows, _, comps, block, _ = dipole.shape
    first = state is None
    low_blocks = sum(p.shape[0] for p in pieces) + 1
    n_slots = min(SLOTS, layout[0])
    operands = [plan, dipole, *pieces, *needed]
    in_specs = [ANY] * len(operands)
    aliases = {}
    if not first:
        aliases = {len(operands): 0, len(operands) + 1: 1}
        operands += list(state)
        in_specs += [VMEM, VMEM]
    entries = layout[0] / 16
    result = pl.pallas_call(
        functools.partial(stage_body, stage, first, reach, layout, len(pieces), len(needed)),
        out_shape=[
            pltpu.VMEM((rows, comps * block, lower_count), jnp.float32),
            pltpu.VMEM((n_slots, comps, block, block), jnp.bfloat16),
            jax.ShapeDtypeStruct((8, 128), jnp.float32),
        ],
        in_specs=in_specs,
        out_specs=[VMEM, VMEM, ANY],
        input_output_aliases=aliases,
        scratch_shapes=[
            pltpu.SMEM(plan.shape, jnp.int32),
            pltpu.VMEM((low_blocks, block, lower_count), jnp.bfloat16),
            pltpu.SemaphoreType.DMA,
            pltpu.SemaphoreType.DMA((n_slots,)),
            pltpu.SemaphoreType.DMA((max(len(pieces), 1),)),
        ],
        cost_estimate=pl.CostEstimate(
            flops=int(entries * comps * block * block * lower_count * 2),
            bytes_accessed=int(entries * comps * block * block * 2),
            transcendentals=0,
        ),
        compiler_params=pltpu.CompilerParams(vmem_limit_bytes=(8 if low_blocks < 64 else 30) * 2**20),
    )(*operands)
    return result[:2], result[2]


def after(done, array):
    return pl.pallas_call(
        lambda *refs: None,
        out_shape=jax.ShapeDtypeStruct(array.shape, array.dtype),
        in_specs=[ANY, ANY],
        out_specs=ANY,
        input_output_aliases={0: 0},
        compiler_params=pltpu.CompilerParams(has_side_effects=True, vmem_limit_bytes=2**20),
    )(array, done)


def sorted_entries(stage, slot, n_stages, low_bits):
    rows, count = stage.shape
    total = rows * count
    row = lax.broadcasted_iota(jnp.int32, stage.shape, 0)
    entry = lax.broadcasted_iota(jnp.int32, stage.shape, 1)
    code = ((((row << ENTRY_BITS) + entry) << low_bits) + slot).reshape(total)
    key = (stage * total + row * count + entry).reshape(total)
    rank = jnp.sum((key[None, :] < key[:, None]).astype(jnp.int32), axis=1)
    length = -(-(total + n_stages + 1) // 128) * 128
    place = jnp.arange(length, dtype=jnp.int32)
    codes = jnp.sum(jnp.where(rank[:, None] == place[None, :], code[:, None], 0), axis=0)
    bounds = jnp.sum((stage.reshape(total, 1) < place[None, :] - total).astype(jnp.int32), axis=0)
    return jnp.where(place < total, codes, bounds)


def ring_moments(dipole, block_cols, lower_blocks, group, needed):
    rows = dipole.shape[0]
    lower_count = lower_blocks.shape[2]
    me = lax.axis_index("blk")
    chips = group // 2
    order = [c for c in range(0, chips, 2)] + [c for c in range(chips - 1, 0, -2)]
    steps = [(order[i], order[(i + 1) % chips]) for i in range(chips)]
    ways = [
        [(2 * a, 2 * b) for a, b in steps] + [(2 * b + 1, 2 * a + 1) for a, b in steps],
        [(2 * b, 2 * a) for a, b in steps] + [(2 * a + 1, 2 * b + 1) for a, b in steps],
    ]
    sibling = [(d, d ^ 1) for d in range(group)]
    half = rows // 2

    def position(device):
        chip = device // 2
        return jnp.where(chip % 2 == 0, chip // 2, chips - 1 - chip // 2)

    owner = block_cols // rows
    local = block_cols % rows
    part = local // half
    forward = (part + owner) % 2 == 0
    mine, theirs = position(me), position(owner)
    hops = jnp.where(forward, mine - theirs, theirs - mine) % chips
    other_core = (owner + me) % 2
    stage = jnp.where(hops == 0, 1, 2 * hops + part)
    slot = jnp.where(hops == 0, other_core * rows + local, other_core * half + local % half)
    n_stages = 2 * chips
    layout = (block_cols.size, (2 * rows - 1).bit_length())
    plan = sorted_entries(stage, slot, n_stages, layout[1])
    reach = [FIRST_SLOTS] + [SLOTS] * (n_stages - 1)

    def hop(array, p):
        return lax.ppermute(array, "blk", ways[p])

    def cross(array):
        return [array, lax.ppermute(array, "blk", sibling)]

    def compute(number, arrived, state, needed=()):
        return run_stage(number, reach, plan, layout, dipole, arrived, lower_count, state, needed)

    flying = [hop(lower_blocks[p * half : (p + 1) * half], p) for p in range(2)]
    waiting = (1, cross(lower_blocks))
    state, done = compute(0, [], None, needed)
    for h in range(1, chips):
        for p in range(2):
            here = after(done, flying[p])
            if h < chips - 1:
                flying[p] = hop(here, p)
            here = cross(here)
            state, done = compute(*waiting, state)
            waiting = (2 * h + p, here)
    state, done = compute(*waiting, state)
    return state[0]


def gathered_moments(dipole, block_cols, lower_blocks):
    gathered = lax.all_gather(lower_blocks, "blk", axis=0, tiled=True)
    layout = (block_cols.size, (gathered.shape[0] - 1).bit_length())
    plan = sorted_entries(jnp.zeros_like(block_cols), block_cols, 1, layout[1])
    state, _ = run_stage(0, [SLOTS], plan, layout, dipole, [gathered], lower_blocks.shape[2], None)
    return state[0]


def own_rows(proj, group):
    me = lax.axis_index("blk")
    comps, upper_count, lower_count = proj.shape
    share = upper_count // group
    held = proj.reshape(comps, group, share, lower_count)
    bit = 1
    while bit < group:
        halves = held.reshape(comps, held.shape[1] // 2, 2, share, lower_count)
        side = (me // bit) % 2
        keep = lax.dynamic_index_in_dim(halves, side, 2, keepdims=False)
        send = lax.dynamic_index_in_dim(halves, 1 - side, 2, keepdims=False)
        held = keep + lax.ppermute(send, "blk", [(d, d ^ bit) for d in range(group)])
        bit *= 2
    return held[:, 0]


def per_device(dipole, block_cols, upper_vecs, lower_vecs, upper_energy, lower_energy):
    rows, _, _, block, _ = dipole.shape
    group = lax.axis_size("blk")
    me = lax.axis_index("blk")
    lower_blocks = lower_vecs.reshape(rows, block, lower_vecs.shape[1])
    upper_t = upper_vecs.T
    share = upper_vecs.shape[1] // group
    energy = lax.dynamic_slice_in_dim(upper_energy, me * share, share, 0)
    wavenumber = energy[:, None] - lower_energy[None, :]
    factor = wavenumber**3 * jnp.exp(-lower_energy / THERMAL)[None, :]
    comps = dipole.shape[2]
    if rows % 2 == 0 and share % 8 == 0 and group >= 8 and group & (group - 1) == 0:
        levels = jnp.arange(group.bit_length() - 1, dtype=jnp.int32)
        bits = jnp.broadcast_to(((me >> levels) & 1)[:, None, None], (levels.shape[0], 8, 128))
        needed = [upper_t, factor, bits]
        moments = ring_moments(dipole, block_cols, lower_blocks, group, needed)
        return own_outputs(upper_t, moments, comps, bits, factor, group)
    moments = gathered_moments(dipole, block_cols, lower_blocks)

    def body(upper_t, moments, proj):
        proj[...] = project(upper_t, moments, comps, (upper_t.shape[0],))

    shape = jax.ShapeDtypeStruct((comps, upper_t.shape[0], lower_blocks.shape[2]), jnp.float32)
    own = own_rows(small_call(body, shape, upper_t, moments), group)
    strength = jnp.sum(own * own, axis=0)
    return strength, factor * strength


def solution(mesh):
    placed = (
        P("blk", None, None, None, None),
        P("blk", None),
        P(("jpair", "blk"), None),
        P(("jpair", "blk"), None),
        P("jpair"),
        P("jpair"),
    )
    return jax.shard_map(
        per_device,
        mesh=mesh,
        in_specs=placed,
        out_specs=(P(("jpair", "blk"), None), P(("jpair", "blk"), None)),
        check_vma=False,
    )
```

```python
import functools

import jax
import jax.numpy as jnp
from jax import lax
from jax.experimental import pallas as pl
from jax.experimental.pallas import tpu as pltpu
from jax.sharding import PartitionSpec as P

THERMAL = 0.3
SLOTS = 32
FIRST_SLOTS = 20
GROUP = 4
ENTRY_BITS = 5

VMEM = pl.BlockSpec(memory_space=pltpu.VMEM)
SMEM = pl.BlockSpec(memory_space=pltpu.SMEM)
ANY = pl.BlockSpec(memory_space=pl.ANY)


def stage_body(stage, first, reach, layout, n_pieces, n_behind, *refs):
    plan, dipole = refs[:2]
    pieces = refs[2 : 2 + n_pieces]
    refs = refs[2 + n_pieces + n_behind :]
    if not first:
        refs = refs[2:]
    moments, entries, _, entry_sems = refs
    n_slots, comps, block, _ = entries.shape
    total, low_bits = layout
    low_mask = (1 << low_bits) - 1

    begin = plan[total + stage]
    end = plan[total + stage + 1]
    ahead = jnp.minimum(begin + reach[stage], total)
    if first:
        ready = begin
    else:
        ready = jnp.maximum(jnp.minimum(plan[total + stage - 1] + reach[stage - 1], total), begin)

    def place(pos):
        return pos & (n_slots - 1) if n_slots & (n_slots - 1) == 0 else lax.rem(pos, n_slots)

    def row(code):
        return code >> (low_bits + 1 + ENTRY_BITS)

    def load(pos):
        code = plan[pos]
        slot = place(pos)
        entry = (code >> (low_bits + 1)) & ((1 << ENTRY_BITS) - 1)
        return pltpu.make_async_copy(dipole.at[row(code), entry], entries.at[slot], entry_sems.at[slot])

    @pl.loop(ready, ahead)
    def _(pos):
        load(pos).start()

    if first:
        moments[...] = jnp.zeros_like(moments)

    def lower_block(code):
        index = code & low_mask
        if len(pieces) == 1:
            return pieces[0][index]
        return jnp.where((code >> low_bits) & 1 == 1, pieces[1][index], pieces[0][index])

    def work(start):
        positions = [start + i for i in range(GROUP)]

        @pl.when(start + GROUP > ready)
        def _():
            for pos in positions:
                @pl.when((pos >= ready) & (pos < end))
                def _(pos=pos):
                    load(pos).wait()

        kept = [jnp.minimum(pos, end - 1) for pos in positions]
        codes = [plan[pos] for pos in kept]
        rows = [row(code) for code in codes]
        blocks = [
            jnp.where(pos < end, lower_block(code), 0).astype(jnp.bfloat16)
            for pos, code in zip(positions, codes)
        ]
        for a in range(comps):
            products = [
                jnp.dot(entries[place(pos), a], lower, preferred_element_type=jnp.float32)
                for pos, lower in zip(kept, blocks)
            ]
            for r, product in zip(rows, products):
                moments[r, pl.ds(a * block, block)] += product

        @pl.when(start + n_slots < end)
        def _():
            for pos in positions:
                @pl.when(pos + n_slots < end)
                def _(pos=pos):
                    load(pos + n_slots).start()

    if pieces:
        @pl.loop(0, (end - begin + GROUP - 1) // GROUP)
        def _(g):
            work(begin + g * GROUP)

    @pl.loop(jnp.maximum(ready, end), ahead)
    def _(pos):
        load(pos).wait()


def split_parts(sums, bits, levels, parts):
    comps, count, share, lower_count = sums.shape
    pieces = [sums]
    for level in levels:
        side = jnp.broadcast_to(
            bits[level][None, None, :1], (comps, pieces[0].shape[1] // 2, share, lower_count)
        ) > 0
        same, other = [], []
        for piece in pieces:
            halves = piece.reshape(comps, piece.shape[1] // 2, 2, share, lower_count)
            same.append(jnp.where(side, halves[:, :, 1], halves[:, :, 0]))
            other.append(jnp.where(side, halves[:, :, 0], halves[:, :, 1]))
        pieces = same + other
    for piece, part in zip(pieces, parts):
        part[...] = piece


def project(upper_t, moments, comps, lay):
    rows, height, _ = moments.shape
    block = height // comps
    span = min(4, rows)
    sums = []
    for a in range(comps):
        acc = None
        for r in range(0, rows, span):
            parts = [moments[r + i, pl.ds(a * block, block)] for i in range(span)]
            wide = jnp.concatenate(parts, axis=0)
            high = wide.astype(jnp.bfloat16)
            rest = (wide - high.astype(jnp.float32)).astype(jnp.bfloat16)
            both = jnp.concatenate([high, rest], axis=1)
            term = jnp.dot(
                upper_t[:, pl.ds(r * block, span * block)], both, preferred_element_type=jnp.float32
            )
            acc = term if acc is None else acc + term
        half = acc.shape[1] // 2
        sums.append((acc[:, :half] + acc[:, half:]).reshape(lay + (half,)))
    return jnp.stack(sums)


def small_call(body, out_shape, *operands):
    return pl.pallas_call(
        body,
        out_shape=out_shape,
        in_specs=[VMEM] * len(operands),
        out_specs=jax.tree.map(lambda _: VMEM, out_shape),
        compiler_params=pltpu.CompilerParams(vmem_limit_bytes=8 * 2**20),
    )(*operands)


def own_outputs(upper_t, moments, comps, bits, factor, group):
    upper_count = upper_t.shape[0]
    lower_count = moments.shape[2]
    share = upper_count // group
    levels = bits.shape[0]

    rounds = [[0]] + [list(range(i, min(i + 2, levels))) for i in range(1, levels, 2)]
    left = group

    def shapes(number):
        count = left >> len(rounds[number])
        return [jax.ShapeDtypeStruct((comps, count, share, lower_count), jnp.float32)] * (
            1 << len(rounds[number])
        )

    def first(upper_t, moments, bits, *parts):
        split_parts(project(upper_t, moments, comps, (group, share)), bits, rounds[0], parts)

    def middle(number, n_sums, *refs):
        total = refs[0][...]
        for ref in refs[1:n_sums]:
            total = total + ref[...]
        split_parts(total, refs[n_sums], rounds[number], refs[n_sums + 1 :])

    def final(n_sums, *refs):
        total = refs[0][...]
        for ref in refs[1:n_sums]:
            total = total + ref[...]
        factor, strength, intensity = refs[n_sums:]
        own = total[:, 0]
        strength[...] = jnp.sum(own * own, axis=0)
        intensity[...] = factor[...] * strength[...]

    parts = small_call(first, shapes(0), upper_t, moments, bits)
    for number, used in enumerate(rounds):
        left >>= len(used)
        terms = [parts[0]]
        for choice in range(1, len(parts)):
            mask = sum(1 << level for i, level in enumerate(used) if (choice >> i) & 1)
            terms.append(lax.ppermute(parts[choice], "blk", [(d, d ^ mask) for d in range(group)]))
        if number + 1 < len(rounds):
            parts = small_call(
                functools.partial(middle, number + 1, len(terms)), shapes(number + 1), *terms, bits
            )
    out = [jax.ShapeDtypeStruct((share, lower_count), jnp.float32)] * 2
    return small_call(functools.partial(final, len(terms)), out, *terms, factor)


def run_stage(stage, reach, plan, layout, dipole, pieces, lower_count, state, behind=()):
    rows, _, comps, block, _ = dipole.shape
    first = state is None
    low_blocks = sum(p.shape[0] for p in pieces)
    n_slots = min(SLOTS, layout[0])
    operands = [plan, dipole, *pieces, *behind]
    in_specs = [SMEM, ANY] + [VMEM] * len(pieces) + [ANY] * len(behind)
    aliases = {}
    if not first:
        aliases = {len(operands): 0, len(operands) + 1: 1}
        operands += list(state)
        in_specs += [VMEM, VMEM]
    entries = layout[0] / 16
    result = pl.pallas_call(
        functools.partial(stage_body, stage, first, reach, layout, len(pieces), len(behind)),
        out_shape=[
            pltpu.VMEM((rows, comps * block, lower_count), jnp.float32),
            pltpu.VMEM((n_slots, comps, block, block), jnp.bfloat16),
            jax.ShapeDtypeStruct((8, 128), jnp.float32),
        ],
        in_specs=in_specs,
        out_specs=[VMEM, VMEM, ANY],
        input_output_aliases=aliases,
        scratch_shapes=[
            pltpu.SemaphoreType.DMA((n_slots,)),
        ],
        cost_estimate=pl.CostEstimate(
            flops=int(entries * comps * block * block * lower_count * 2),
            bytes_accessed=int(entries * comps * block * block * 2),
            transcendentals=0,
        ),
        compiler_params=pltpu.CompilerParams(vmem_limit_bytes=(8 if low_blocks < 64 else 40) * 2**20),
    )(*operands)
    return result[:2], result[2]


def after(done, *arrays):
    count = len(arrays)
    return pl.pallas_call(
        lambda *refs: None,
        out_shape=[jax.ShapeDtypeStruct(x.shape, x.dtype) for x in arrays],
        in_specs=[ANY] * (count + 1),
        out_specs=[ANY] * count,
        input_output_aliases={i: i for i in range(count)},
        compiler_params=pltpu.CompilerParams(has_side_effects=True, vmem_limit_bytes=2**20),
    )(*arrays, done)


def transposed(array, behind):
    rows, columns = array.shape
    step = min(rows, columns)

    def body(source, _, target):
        for i in range(0, rows, step):
            target[:, pl.ds(i, step)] = source[pl.ds(i, step), :].T

    return pl.pallas_call(
        body,
        out_shape=jax.ShapeDtypeStruct((columns, rows), array.dtype),
        in_specs=[VMEM, ANY],
        out_specs=VMEM,
        compiler_params=pltpu.CompilerParams(vmem_limit_bytes=8 * 2**20),
    )(array, behind)


def part_of(array, start, count, *needed):
    def body(*refs):
        pltpu.sync_copy(refs[0].at[pl.ds(start, count)], refs[-1])

    return pl.pallas_call(
        body,
        out_shape=jax.ShapeDtypeStruct((count,) + array.shape[1:], array.dtype),
        in_specs=[pl.BlockSpec(memory_space=pltpu.HBM)] + [SMEM] * len(needed),
        out_specs=ANY,
        compiler_params=pltpu.CompilerParams(vmem_limit_bytes=2**20),
    )(array, *needed)


def sorted_entries(stage, slot, n_stages, low_bits):
    rows, count = stage.shape
    total = rows * count
    row = lax.broadcasted_iota(jnp.int32, stage.shape, 0)
    entry = lax.broadcasted_iota(jnp.int32, stage.shape, 1)
    code = ((((row << ENTRY_BITS) + entry) << (low_bits + 1)) + slot).reshape(total)
    key = (stage * total + row * count + entry).reshape(total)
    rank = jnp.sum((key[None, :] < key[:, None]).astype(jnp.int32), axis=1)
    length = -(-(total + n_stages + 1) // 128) * 128
    place = jnp.arange(length, dtype=jnp.int32)
    codes = jnp.sum(jnp.where(rank[:, None] == place[None, :], code[:, None], 0), axis=0)
    bounds = jnp.sum((stage.reshape(total, 1) < place[None, :] - total).astype(jnp.int32), axis=0)
    return pl.pallas_call(
        lambda source, plan: pltpu.sync_copy(source, plan),
        out_shape=pltpu.SMEM((length,), jnp.int32),
        in_specs=[ANY],
        out_specs=SMEM,
        compiler_params=pltpu.CompilerParams(vmem_limit_bytes=2**20),
    )(jnp.where(place < total, codes, bounds))


def ring_moments(dipole, block_cols, lower_blocks, upper_vecs, group, needed):
    rows = dipole.shape[0]
    lower_count = lower_blocks.shape[2]
    me = lax.axis_index("blk")
    chips = group // 2
    order = [c for c in range(0, chips, 2)] + [c for c in range(chips - 1, 0, -2)]
    steps = [(order[i], order[(i + 1) % chips]) for i in range(chips)]
    ways = [
        [(2 * a, 2 * b) for a, b in steps] + [(2 * b + 1, 2 * a + 1) for a, b in steps],
        [(2 * b, 2 * a) for a, b in steps] + [(2 * a + 1, 2 * b + 1) for a, b in steps],
    ]
    sibling = [(d, d ^ 1) for d in range(group)]
    half = rows // 2

    def position(device):
        chip = device // 2
        return jnp.where(chip % 2 == 0, chip // 2, chips - 1 - chip // 2)

    owner = block_cols // rows
    local = block_cols % rows
    part = local // half
    forward = (part + owner) % 2 == 0
    mine, theirs = position(me), position(owner)
    hops = jnp.where(forward, mine - theirs, theirs - mine) % chips
    other_core = (owner + me) % 2
    stage = 1 + jnp.where(hops == 0, other_core, 2 * hops + part)
    index = jnp.where(hops == 0, local, local % half)
    n_stages = 2 * chips + 1
    layout = (block_cols.size, (rows - 1).bit_length())
    plan = sorted_entries(stage, (other_core << layout[1]) + index, n_stages, layout[1])
    reach = [FIRST_SLOTS] + [SLOTS] * (n_stages - 1)

    def hop(array, p):
        return lax.ppermute(array, "blk", ways[p])

    def cross(array):
        return lax.ppermute(array, "blk", sibling)

    def compute(number, arrived, state, *behind):
        return run_stage(number, reach, plan, layout, dipole, arrived, lower_count, state, behind)

    flying = [hop(part_of(lower_blocks, 0, half), 0)]
    there = cross(lower_blocks)
    second = part_of(lower_blocks, half, half, plan)
    flying.append(hop(second, 1))
    waiting = [(1, [lower_blocks]), (2, [there])]
    state, done = compute(0, [], None, second, *needed)
    upper_t = None
    for h in range(1, chips):
        for p in range(2):
            here = after(done, flying[p])[0]
            if h < chips - 1:
                flying[p] = hop(here, p)
            waiting.append((2 * h + p + 1, [here, cross(here)]))
            for _ in range(2 if (h, p) == (1, 0) else 1):
                state, done = compute(*waiting.pop(0), state, here)
            if upper_t is None and 2 * h >= chips:
                done = upper_t = transposed(upper_vecs, done)
    for number, arrived in waiting:
        state, done = compute(number, arrived, state)
    return state[0], upper_t


def gathered_moments(dipole, block_cols, lower_blocks):
    gathered = lax.all_gather(lower_blocks, "blk", axis=0, tiled=True)
    layout = (block_cols.size, (gathered.shape[0] - 1).bit_length())
    plan = sorted_entries(jnp.zeros_like(block_cols), block_cols, 1, layout[1])
    state, _ = run_stage(0, [SLOTS], plan, layout, dipole, [gathered], lower_blocks.shape[2], None)
    return state[0]


def own_rows(proj, group):
    me = lax.axis_index("blk")
    comps, upper_count, lower_count = proj.shape
    share = upper_count // group
    held = proj.reshape(comps, group, share, lower_count)
    bit = 1
    while bit < group:
        halves = held.reshape(comps, held.shape[1] // 2, 2, share, lower_count)
        side = (me // bit) % 2
        keep = lax.dynamic_index_in_dim(halves, side, 2, keepdims=False)
        send = lax.dynamic_index_in_dim(halves, 1 - side, 2, keepdims=False)
        held = keep + lax.ppermute(send, "blk", [(d, d ^ bit) for d in range(group)])
        bit *= 2
    return held[:, 0]


def per_device(dipole, block_cols, upper_vecs, lower_vecs, upper_energy, lower_energy):
    rows, _, _, block, _ = dipole.shape
    group = lax.axis_size("blk")
    me = lax.axis_index("blk")
    lower_blocks = lower_vecs.reshape(rows, block, lower_vecs.shape[1])
    share = upper_vecs.shape[1] // group
    energy = lax.dynamic_slice_in_dim(upper_energy, me * share, share, 0)
    wavenumber = energy[:, None] - lower_energy[None, :]
    factor = wavenumber**3 * jnp.exp(-lower_energy / THERMAL)[None, :]
    comps = dipole.shape[2]
    if rows % 2 == 0 and share % 8 == 0 and group >= 8 and group & (group - 1) == 0:
        levels = jnp.arange(group.bit_length() - 1, dtype=jnp.int32)
        bits = jnp.broadcast_to(((me >> levels) & 1)[:, None, None], (levels.shape[0], 8, 128))
        moments, upper_t = ring_moments(
            dipole, block_cols, lower_blocks, upper_vecs, group, [factor, bits]
        )
        return own_outputs(upper_t, moments, comps, bits, factor, group)
    moments = gathered_moments(dipole, block_cols, lower_blocks)
    upper_t = upper_vecs.T

    def body(upper_t, moments, proj):
        proj[...] = project(upper_t, moments, comps, (upper_t.shape[0],))

    shape = jax.ShapeDtypeStruct((comps, upper_t.shape[0], lower_blocks.shape[2]), jnp.float32)
    own = own_rows(small_call(body, shape, upper_t, moments), group)
    strength = jnp.sum(own * own, axis=0)
    return strength, factor * strength


def solution(mesh):
    placed = (
        P("blk", None, None, None, None),
        P("blk", None),
        P(("jpair", "blk"), None),
        P(("jpair", "blk"), None),
        P("jpair"),
        P("jpair"),
    )
    return jax.shard_map(
        per_device,
        mesh=mesh,
        in_specs=placed,
        out_specs=(P(("jpair", "blk"), None), P(("jpair", "blk"), None)),
        check_vma=False,
    )
```

```python
import functools

import jax
import jax.numpy as jnp
from jax import lax
from jax.experimental import pallas as pl
from jax.experimental.pallas import tpu as pltpu
from jax.sharding import PartitionSpec as P

THERMAL = 0.3
LANES = 128
SLOTS = 32
FIRST_SLOTS = 20
GROUP = 6
ENTRY_BITS = 5

VMEM = pl.BlockSpec(memory_space=pltpu.VMEM)
SMEM = pl.BlockSpec(memory_space=pltpu.SMEM)
ANY = pl.BlockSpec(memory_space=pl.ANY)


def stage_body(stage, first, reach, layout, n_pieces, n_behind, *refs):
    plan, dipole = refs[:2]
    pieces = refs[2 : 2 + n_pieces]
    refs = refs[2 + n_pieces + n_behind :]
    if not first:
        refs = refs[2:]
    moments, entries, _, entry_sems = refs
    n_slots, comps, block, _ = entries.shape
    total, low_bits = layout
    low_mask = (1 << low_bits) - 1

    begin = plan[total + stage]
    end = plan[total + stage + 1]
    ahead = jnp.minimum(begin + reach[stage], total)
    if first:
        ready = begin
    else:
        ready = jnp.maximum(jnp.minimum(plan[total + stage - 1] + reach[stage - 1], total), begin)

    def place(pos):
        return pos & (n_slots - 1) if n_slots & (n_slots - 1) == 0 else lax.rem(pos, n_slots)

    def row(code):
        return code >> (low_bits + 1 + ENTRY_BITS)

    def load(pos):
        code = plan[pos]
        slot = place(pos)
        entry = (code >> (low_bits + 1)) & ((1 << ENTRY_BITS) - 1)
        return pltpu.make_async_copy(dipole.at[row(code), entry], entries.at[slot], entry_sems.at[slot])

    @pl.loop(ready, ahead)
    def _(pos):
        load(pos).start()

    if first:
        moments[...] = jnp.zeros_like(moments)

    def lower_block(code):
        index = code & low_mask
        if len(pieces) == 1:
            return pieces[0][index]
        return jnp.where((code >> low_bits) & 1 == 1, pieces[1][index], pieces[0][index])

    def work(start):
        positions = [start + i for i in range(GROUP)]

        @pl.when(start + GROUP > ready)
        def _():
            for pos in positions:
                @pl.when((pos >= ready) & (pos < end))
                def _(pos=pos):
                    load(pos).wait()

        kept = [jnp.minimum(pos, end - 1) for pos in positions]
        codes = [plan[pos] for pos in kept]
        rows = [row(code) for code in codes]
        blocks = [
            jnp.where(pos < end, lower_block(code), 0).astype(jnp.bfloat16)
            for pos, code in zip(positions, codes)
        ]
        for a in range(comps):
            products = [
                jnp.dot(entries[place(pos), a], lower, preferred_element_type=jnp.float32)
                for pos, lower in zip(kept, blocks)
            ]
            for r, product in zip(rows, products):
                moments[r, pl.ds(a * block, block)] += product

        @pl.when(start + n_slots < end)
        def _():
            for pos in positions:
                @pl.when(pos + n_slots < end)
                def _(pos=pos):
                    load(pos + n_slots).start()

    if pieces:
        @pl.loop(0, (end - begin + GROUP - 1) // GROUP)
        def _(g):
            work(begin + g * GROUP)

    @pl.loop(jnp.maximum(ready, end), ahead)
    def _(pos):
        load(pos).wait()


def split_parts(sums, me, levels, parts):
    comps, count, share, lower_count = sums.shape
    pieces = [sums]
    for level in levels:
        side = ((me >> level) & 1) == 1
        same, other = [], []
        for piece in pieces:
            halves = piece.reshape(comps, piece.shape[1] // 2, 2, share, lower_count)
            same.append(jnp.where(side, halves[:, :, 1], halves[:, :, 0]))
            other.append(jnp.where(side, halves[:, :, 0], halves[:, :, 1]))
        pieces = same + other
    for piece, part in zip(pieces, parts):
        part[...] = piece


def project(upper_t, moments, comps, lay):
    rows, height, _ = moments.shape
    block = height // comps
    span = min(4, rows)
    sums = []
    for a in range(comps):
        acc = None
        for r in range(0, rows, span):
            parts = [moments[r + i, pl.ds(a * block, block)] for i in range(span)]
            wide = jnp.concatenate(parts, axis=0)
            high = wide.astype(jnp.bfloat16)
            rest = (wide - high.astype(jnp.float32)).astype(jnp.bfloat16)
            both = jnp.concatenate([high, rest], axis=1)
            term = jnp.dot(
                upper_t[:, pl.ds(r * block, span * block)], both, preferred_element_type=jnp.float32
            )
            acc = term if acc is None else acc + term
        half = acc.shape[1] // 2
        sums.append((acc[:, :half] + acc[:, half:]).reshape(lay + (half,)))
    return jnp.stack(sums)


def small_call(body, out_shape, *operands, scalars=()):
    return pl.pallas_call(
        body,
        out_shape=out_shape,
        in_specs=[SMEM] * len(scalars) + [VMEM] * len(operands),
        out_specs=jax.tree.map(lambda _: VMEM, out_shape),
        compiler_params=pltpu.CompilerParams(vmem_limit_bytes=8 * 2**20),
    )(*scalars, *operands)


def own_outputs(upper_t, moments, comps, plan, spot, upper_energy, lower_energy, group):
    upper_count = upper_t.shape[0]
    lower_count = moments.shape[2]
    share = upper_count // group
    levels = group.bit_length() - 1

    rounds = [[0]] + [list(range(i, min(i + 2, levels))) for i in range(1, levels, 2)]
    left = group

    def shapes(number):
        count = left >> len(rounds[number])
        return [jax.ShapeDtypeStruct((comps, count, share, lower_count), jnp.float32)] * (
            1 << len(rounds[number])
        )

    def first(plan, upper_t, moments, *parts):
        split_parts(project(upper_t, moments, comps, (group, share)), plan[spot], rounds[0], parts)

    def total(refs):
        result = refs[0][...]
        for ref in refs[1:]:
            result = result + ref[...]
        return result

    def middle(number, n_sums, plan, *refs):
        split_parts(total(refs[:n_sums]), plan[spot], rounds[number], refs[n_sums:])

    def final(n_sums, plan, *refs):
        own = total(refs[:n_sums])[:, 0]
        upper, lower, strength, intensity = refs[n_sums:]
        strength[...] = jnp.sum(own * own, axis=0)
        row = plan[spot] * share + lax.broadcasted_iota(jnp.int32, (share, LANES), 0)
        lane = lax.broadcasted_iota(jnp.int32, (share, LANES), 1)
        energy = jnp.zeros((share, LANES), jnp.float32)
        for start in range(0, upper_count, LANES):
            energy += jnp.where(row == lane + start, upper[pl.ds(start, LANES)].reshape(1, LANES), 0.0)
        below = lower[...].reshape(1, lower_count)
        wavenumber = jnp.sum(energy, axis=1, keepdims=True) - below
        intensity[...] = wavenumber**3 * jnp.exp(-below / THERMAL) * strength[...]

    parts = small_call(first, shapes(0), upper_t, moments, scalars=(plan,))
    for number, used in enumerate(rounds):
        left >>= len(used)
        terms = [parts[0]]
        for choice in range(1, len(parts)):
            mask = sum(1 << level for i, level in enumerate(used) if (choice >> i) & 1)
            terms.append(lax.ppermute(parts[choice], "blk", [(d, d ^ mask) for d in range(group)]))
        if number + 1 < len(rounds):
            parts = small_call(
                functools.partial(middle, number + 1, len(terms)), shapes(number + 1), *terms, scalars=(plan,)
            )
    out = [jax.ShapeDtypeStruct((share, lower_count), jnp.float32)] * 2
    body = functools.partial(final, len(terms))
    return small_call(body, out, *terms, upper_energy, lower_energy, scalars=(plan,))


def run_stage(stage, reach, plan, layout, dipole, pieces, lower_count, state, behind=()):
    rows, _, comps, block, _ = dipole.shape
    first = state is None
    low_blocks = sum(p.shape[0] for p in pieces)
    n_slots = min(SLOTS, layout[0])
    operands = [plan, dipole, *pieces, *behind]
    in_specs = [SMEM, ANY] + [VMEM] * len(pieces) + [ANY] * len(behind)
    aliases = {}
    if not first:
        aliases = {len(operands): 0, len(operands) + 1: 1}
        operands += list(state)
        in_specs += [VMEM, VMEM]
    entries = layout[0] / 16
    result = pl.pallas_call(
        functools.partial(stage_body, stage, first, reach, layout, len(pieces), len(behind)),
        out_shape=[
            pltpu.VMEM((rows, comps * block, lower_count), jnp.float32),
            pltpu.VMEM((n_slots, comps, block, block), jnp.bfloat16),
            jax.ShapeDtypeStruct((8, 128), jnp.float32),
        ],
        in_specs=in_specs,
        out_specs=[VMEM, VMEM, ANY],
        input_output_aliases=aliases,
        scratch_shapes=[
            pltpu.SemaphoreType.DMA((n_slots,)),
        ],
        cost_estimate=pl.CostEstimate(
            flops=int(entries * comps * block * block * lower_count * 2),
            bytes_accessed=int(entries * comps * block * block * 2),
            transcendentals=0,
        ),
        compiler_params=pltpu.CompilerParams(vmem_limit_bytes=(8 if low_blocks < 64 else 40) * 2**20),
    )(*operands)
    return result[:2], result[2]


def after(done, *arrays):
    count = len(arrays)
    return pl.pallas_call(
        lambda *refs: None,
        out_shape=[jax.ShapeDtypeStruct(x.shape, x.dtype) for x in arrays],
        in_specs=[ANY] * (count + 1),
        out_specs=[ANY] * count,
        input_output_aliases={i: i for i in range(count)},
        compiler_params=pltpu.CompilerParams(has_side_effects=True, vmem_limit_bytes=2**20),
    )(*arrays, done)


def transposed(array, behind):
    rows, columns = array.shape
    step = min(rows, columns)

    def body(source, _, target):
        for i in range(0, rows, step):
            target[:, pl.ds(i, step)] = source[pl.ds(i, step), :].T

    return pl.pallas_call(
        body,
        out_shape=jax.ShapeDtypeStruct((columns, rows), array.dtype),
        in_specs=[VMEM, ANY],
        out_specs=VMEM,
        compiler_params=pltpu.CompilerParams(vmem_limit_bytes=8 * 2**20),
    )(array, behind)


def part_of(array, start, count, *needed):
    def body(*refs):
        pltpu.sync_copy(refs[0].at[pl.ds(start, count)], refs[-1])

    return pl.pallas_call(
        body,
        out_shape=jax.ShapeDtypeStruct((count,) + array.shape[1:], array.dtype),
        in_specs=[ANY] + [SMEM] * len(needed),
        out_specs=ANY,
        compiler_params=pltpu.CompilerParams(vmem_limit_bytes=2**20),
    )(pltpu.with_memory_space_constraint(array, pltpu.HBM), *needed)


def sorted_entries(stage, slot, n_stages, low_bits, me):
    rows, count = stage.shape
    total = rows * count
    row = lax.broadcasted_iota(jnp.int32, stage.shape, 0)
    entry = lax.broadcasted_iota(jnp.int32, stage.shape, 1)
    code = ((((row << ENTRY_BITS) + entry) << (low_bits + 1)) + slot).reshape(total)
    key = (stage * total + row * count + entry).reshape(total)
    rank = jnp.sum((key[None, :] < key[:, None]).astype(jnp.int32), axis=1)
    spot = total + n_stages + 1
    length = -(-(spot + 1) // LANES) * LANES
    place = jnp.arange(length, dtype=jnp.int32)
    codes = jnp.sum(jnp.where(rank[:, None] == place[None, :], code[:, None], 0), axis=0)
    bounds = jnp.sum((stage.reshape(total, 1) < place[None, :] - total).astype(jnp.int32), axis=0)
    return spot, pl.pallas_call(
        lambda source, plan: pltpu.sync_copy(source, plan),
        out_shape=pltpu.SMEM((length,), jnp.int32),
        in_specs=[ANY],
        out_specs=SMEM,
        compiler_params=pltpu.CompilerParams(vmem_limit_bytes=2**20),
    )(jnp.where(place < total, codes, jnp.where(place == spot, me, bounds)))


def ring_moments(dipole, block_cols, lower_blocks, upper_vecs, group):
    rows = dipole.shape[0]
    lower_count = lower_blocks.shape[2]
    me = lax.axis_index("blk")
    chips = group // 2
    order = [c for c in range(0, chips, 2)] + [c for c in range(chips - 1, 0, -2)]
    steps = [(order[i], order[(i + 1) % chips]) for i in range(chips)]
    ways = [
        [(2 * a, 2 * b) for a, b in steps] + [(2 * b + 1, 2 * a + 1) for a, b in steps],
        [(2 * b, 2 * a) for a, b in steps] + [(2 * a + 1, 2 * b + 1) for a, b in steps],
    ]
    sibling = [(d, d ^ 1) for d in range(group)]
    half = rows // 2

    def position(device):
        chip = device // 2
        return jnp.where(chip % 2 == 0, chip // 2, chips - 1 - chip // 2)

    owner = block_cols // rows
    local = block_cols % rows
    part = local // half
    forward = (part + owner) % 2 == 0
    mine, theirs = position(me), position(owner)
    hops = jnp.where(forward, mine - theirs, theirs - mine) % chips
    other_core = (owner + me) % 2
    stage = 1 + jnp.where(hops == 0, other_core, 2 * hops + part)
    other = jnp.where(hops == 0, part, other_core)
    n_stages = 2 * chips + 1
    layout = (block_cols.size, (half - 1).bit_length())
    spot, plan = sorted_entries(stage, (other << layout[1]) + local % half, n_stages, layout[1], me)
    reach = [FIRST_SLOTS] + [SLOTS] * (n_stages - 1)

    def hop(array, p):
        return lax.ppermute(array, "blk", ways[p])

    def cross(array):
        return lax.ppermute(array, "blk", sibling)

    def compute(number, arrived, state, *behind):
        return run_stage(number, reach, plan, layout, dipole, arrived, lower_count, state, behind)

    first = part_of(lower_blocks, 0, half)
    flying = [hop(first, 0)]
    there = [cross(first)]
    second = part_of(lower_blocks, half, half, plan)
    flying.append(hop(second, 1))
    there.append(cross(second))
    waiting = [(1, [first, second]), (2, there)]
    state, done = compute(0, [], None, second)
    upper_t = None
    for h in range(1, chips):
        for p in range(2):
            here = after(done, flying[p])[0]
            if h < chips - 1:
                flying[p] = hop(here, p)
            waiting.append((2 * h + p + 1, [here, cross(here)]))
            for _ in range(2 if (h, p) == (1, 0) else 1):
                state, done = compute(*waiting.pop(0), state, here)
            if upper_t is None and 2 * h >= chips:
                done = upper_t = transposed(upper_vecs, done)
    for number, arrived in waiting:
        state, done = compute(number, arrived, state)
    return state[0], upper_t, spot, plan


def gathered_moments(dipole, block_cols, lower_blocks):
    gathered = lax.all_gather(lower_blocks, "blk", axis=0, tiled=True)
    layout = (block_cols.size, (gathered.shape[0] - 1).bit_length())
    _, plan = sorted_entries(jnp.zeros_like(block_cols), block_cols, 1, layout[1], 0)
    state, _ = run_stage(0, [SLOTS], plan, layout, dipole, [gathered], lower_blocks.shape[2], None)
    return state[0]


def own_rows(proj, group):
    me = lax.axis_index("blk")
    comps, upper_count, lower_count = proj.shape
    share = upper_count // group
    held = proj.reshape(comps, group, share, lower_count)
    bit = 1
    while bit < group:
        halves = held.reshape(comps, held.shape[1] // 2, 2, share, lower_count)
        side = (me // bit) % 2
        keep = lax.dynamic_index_in_dim(halves, side, 2, keepdims=False)
        send = lax.dynamic_index_in_dim(halves, 1 - side, 2, keepdims=False)
        held = keep + lax.ppermute(send, "blk", [(d, d ^ bit) for d in range(group)])
        bit *= 2
    return held[:, 0]


def per_device(dipole, block_cols, upper_vecs, lower_vecs, upper_energy, lower_energy):
    rows, _, _, block, _ = dipole.shape
    group = lax.axis_size("blk")
    me = lax.axis_index("blk")
    lower_blocks = lower_vecs.reshape(rows, block, lower_vecs.shape[1])
    share = upper_vecs.shape[1] // group
    comps = dipole.shape[2]
    if rows % 2 == 0 and share % 8 == 0 and upper_vecs.shape[1] % LANES == 0 and group >= 8 and group & (group - 1) == 0:
        moments, upper_t, spot, plan = ring_moments(dipole, block_cols, lower_blocks, upper_vecs, group)
        return own_outputs(upper_t, moments, comps, plan, spot, upper_energy, lower_energy, group)
    energy = lax.dynamic_slice_in_dim(upper_energy, me * share, share, 0)
    wavenumber = energy[:, None] - lower_energy[None, :]
    factor = wavenumber**3 * jnp.exp(-lower_energy / THERMAL)[None, :]
    moments = gathered_moments(dipole, block_cols, lower_blocks)
    upper_t = upper_vecs.T

    def body(upper_t, moments, proj):
        proj[...] = project(upper_t, moments, comps, (upper_t.shape[0],))

    shape = jax.ShapeDtypeStruct((comps, upper_t.shape[0], lower_blocks.shape[2]), jnp.float32)
    own = own_rows(small_call(body, shape, upper_t, moments), group)
    strength = jnp.sum(own * own, axis=0)
    return strength, factor * strength


def solution(mesh):
    placed = (
        P("blk", None, None, None, None),
        P("blk", None),
        P(("jpair", "blk"), None),
        P(("jpair", "blk"), None),
        P("jpair"),
        P("jpair"),
    )
    return jax.shard_map(
        per_device,
        mesh=mesh,
        in_specs=placed,
        out_specs=(P(("jpair", "blk"), None), P(("jpair", "blk"), None)),
        check_vma=False,
    )
```
